32 devices in a mesh: groups: 2 (over y), tensor: 4 (over z), batch: 2 (over x), pool: 2 (over core).
Axes of the slice: x: 2, y: 2, z: 4, core: 2. Of those that a mesh axis runs over, the one named last changes fastest.
Arguments:
- hidden_input: bfloat16 [32, 4, 8192], P(('groups', 'tensor', 'batch', 'pool')), parts along dimension 0, may hold values from -6 to 6
- query_matrix: bfloat16 [8192, 4096], P(None, 'tensor'), may hold values from -0.0625 to 0.0625
- adapter_down_weight: bfloat16 [32, 64, 8192], P(('tensor', 'pool')), may hold values from -0.0625 to 0.0625
- adapter_up_weight: bfloat16 [32, 64, 4096], P(('tensor', 'pool')), may hold values from -0.75 to 0.75
- request_adapter: int32 [32], P(('groups', 'tensor', 'batch', 'pool')), parts along dimension 0, may hold values from 0 to 31
- adapter_slot: int32 [32], replicated, may hold values from 0 to 31, each once
- cached_key_value: bfloat16 [32, 2, 512, 512], P(('groups', 'tensor', 'batch', 'pool')), parts along dimension 0, may hold values from -610 to 610
- fresh_key_value: bfloat16 [32, 2, 4, 512], P(('groups', 'tensor', 'batch', 'pool')), parts along dimension 0, may hold values from -6 to 6
- cached_length: int32 [32], P(('groups', 'tensor', 'batch', 'pool')), parts along dimension 0, may hold values from 2 to 512, as said below
Outputs:
- attention_out: bfloat16 [32, 4, 4096], P(('groups', 'tensor', 'batch', 'pool')), parts along dimension 0
The draws below stay inside these ranges and needn't reach their ends.
There are 2 independent parts, one for each index of `groups`. The reference program is written for one: setup_inputs(seed, part) draws one part's arguments, and reference() takes and returns one part's arrays. A program takes and returns all parts, laid end to end along the dimension named above; an argument that names none is the same for every part. Nothing has to cross between parts.
Inputs may be any that keep to these rules, and one draw needn't show every extreme that they name: Request r attends cached positions 0 to cached_length[r] - 1; some request has exactly 512.
All inputs are finite; a program needn't handle non-finite values.
Results may differ from the reference program's by a relative error of at most 0.012.
The reference program's roundings to bfloat16 on the way count: a program that leaves them out, or rounds other values in their place, can miss the bound.
Values may be sent and summed in bfloat16 or wider, within the bound.
A program may use at most 128 MiB of HBM per device.

```python
import math
import jax
import jax.numpy as jnp
import numpy as np
from jax import lax

MODEL_WIDTH = 8192
QUERY_HEADS = 32
KVH = 4
HEAD_WIDTH = 128
ADAPTER_RANK = 64
STEPS = 4
LEN = 512
REQS = 16
ADAPTER_TOTAL = 32


def draw_cached_key_value(key, part):
    key = jax.random.fold_in(key, 11)
    key_one = jax.random.fold_in(key, 0)
    values_drawn = jnp.clip(jax.random.normal(key_one, (REQS, 2, LEN, KVH * HEAD_WIDTH), jnp.float32), -6.0, 6.0)
    return values_drawn.astype(jnp.bfloat16)


def draw_cached_length(key, part):
    key = jax.random.fold_in(key, 5)
    key_one, key_two = jax.random.split(key, 2)
    lengths = jax.random.randint(key_one, (REQS,), 2, LEN + 1, dtype=jnp.int32)
    longest = jax.random.randint(key_two, (), 0, REQS, dtype=jnp.int32)
    return jnp.where(jnp.arange(REQS, dtype=jnp.int32) == longest, LEN, lengths).astype(jnp.int32)


def place_ends(values, own_key, smallest, largest):
    spot = [jax.random.randint(jax.random.fold_in(own_key, axis), (), 0, length) for axis, length in enumerate(values.shape)]
    widest = values.shape.index(max(values.shape))
    next_to = spot[:widest] + [(spot[widest] + 1) % values.shape[widest]] + spot[widest + 1:]
    return values.at[tuple(spot)].set(smallest).at[tuple(next_to)].set(largest)


def shard_levels(rng, dims, pieces, least, high):
    def one(axis_at, shards_of):
        heights = jax.random.uniform(jax.random.fold_in(jax.random.fold_in(rng, 6), axis_at), (shards_of,), jnp.float32, least / len(pieces), high / len(pieces))
        return jnp.repeat(jnp.exp(heights), dims[axis_at] // shards_of).reshape((-1,) + (1,) * (len(dims) - axis_at - 1))

    level = one(*pieces[0])
    for cut in pieces[1:]:
        level = level * one(*cut)
    return level


def cumulative_ranks(number_of, slope):
    portions = [(1 << 20) // math.isqrt(grade ** slope) + 1 for grade in range(1, number_of + 1)]
    scale = 1 + sum(portions) // (1 << 30)
    return np.cumsum(np.array([max(1, weight // scale) for weight in portions]))


def skewed_ids(key, extent, number_of, skew):
    table = cumulative_ranks(number_of, skew)
    lot = jax.random.randint(jax.random.fold_in(key, 1), extent, 0, int(table[number_of - 1]))
    grade = jnp.searchsorted(jnp.asarray(table, jnp.int32), lot, side="right")
    return jax.random.permutation(jax.random.fold_in(key, 2), number_of)[grade].astype(jnp.int32)


def scatter_about(rng, extent, width, bound, shards=(), held_as=jnp.bfloat16):
    level = shard_levels(rng, extent, shards, -0.22, 0.18) if shards else 1.0
    entries = jax.random.normal(rng, extent, jnp.float32) * width * level
    return jnp.minimum(jnp.maximum(entries, -bound), bound).astype(held_as)


def setup_inputs(seed: int = 0, part: int = 0) -> dict:
    key_list = jax.random.split(jax.random.key(seed), 10)
    part_keys = jax.random.split(jax.random.fold_in(key_list[9], part), 10)
    hidden_input = scatter_about(part_keys[0], (REQS, STEPS, MODEL_WIDTH), 1.0, 6.0, ((0, 16),))
    query_matrix = scatter_about(key_list[1], (MODEL_WIDTH, QUERY_HEADS * HEAD_WIDTH), MODEL_WIDTH ** -0.5, 0.0625, ((1, 4),))
    adapter_down_weight = scatter_about(key_list[2], (ADAPTER_TOTAL, ADAPTER_RANK, MODEL_WIDTH), MODEL_WIDTH ** -0.5, 0.0625, ((0, 8),))
    adapter_up_weight = scatter_about(key_list[3], (ADAPTER_TOTAL, ADAPTER_RANK, QUERY_HEADS * HEAD_WIDTH), ADAPTER_RANK ** -0.5, 0.75, ((0, 8),))
    request_adapter = place_ends(skewed_ids(part_keys[4], (REQS,), ADAPTER_TOTAL, 2), jax.random.fold_in(part_keys[4], 3), 0, ADAPTER_TOTAL - 1).astype(jnp.int32)
    adapter_slot = jax.random.permutation(key_list[5], ADAPTER_TOTAL).astype(jnp.int32)
    cached_key_value = draw_cached_key_value(jax.random.fold_in(jax.random.fold_in(key_list[9], part), 71), part)
    fresh_key_value = scatter_about(part_keys[7], (REQS, 2, STEPS, KVH * HEAD_WIDTH), 1.0, 6.0, ((0, 16),))
    cached_length = draw_cached_length(jax.random.fold_in(jax.random.fold_in(key_list[9], part), 71), part)
    return dict(hidden_input=hidden_input, query_matrix=query_matrix, adapter_down_weight=adapter_down_weight, adapter_up_weight=adapter_up_weight, request_adapter=request_adapter, adapter_slot=adapter_slot, cached_key_value=cached_key_value, fresh_key_value=fresh_key_value, cached_length=cached_length)


def attend(queries, cached_key_value, fresh_key_value, cached_length):
    req_count = queries.shape[0]
    step_count = queries.shape[1]
    cache_size = cached_key_value.shape[2]
    group_size = QUERY_HEADS // KVH
    head_rows = queries.reshape(req_count, step_count, KVH, group_size, HEAD_WIDTH).astype(jnp.float32)
    cache_keys = cached_key_value[:, 0].reshape(req_count, cache_size, KVH, HEAD_WIDTH).astype(jnp.float32)
    cache_values = cached_key_value[:, 1].reshape(req_count, cache_size, KVH, HEAD_WIDTH).astype(jnp.float32)
    new_keys = fresh_key_value[:, 0].reshape(req_count, step_count, KVH, HEAD_WIDTH).astype(jnp.float32)
    new_values = fresh_key_value[:, 1].reshape(req_count, step_count, KVH, HEAD_WIDTH).astype(jnp.float32)
    score_scale = 1.0 / math.sqrt(HEAD_WIDTH)
    cached_scores = jnp.einsum('rskgd,rlkd->rkgsl', head_rows, cache_keys) * score_scale
    fresh_scores = jnp.einsum('rskgd,rtkd->rkgst', head_rows, new_keys) * score_scale
    valid_old = (jnp.arange(cache_size, dtype=jnp.int32)[None, :] < cached_length[:, None])[:, None, None, None, :]
    valid_new = (jnp.arange(step_count, dtype=jnp.int32)[None, :] <= jnp.arange(step_count, dtype=jnp.int32)[:, None])[None, None, None]
    cached_scores = jnp.where(valid_old, cached_scores, -1e+30)
    fresh_scores = jnp.where(valid_new, fresh_scores, -1e+30)
    row_max = jnp.maximum(lax.optimization_barrier(jnp.max(cached_scores, axis=-1)), lax.optimization_barrier(jnp.max(fresh_scores, axis=-1)))[..., None]
    exp_cached = jnp.exp(cached_scores - row_max)
    exp_fresh = jnp.exp(fresh_scores - row_max)
    denominator = lax.optimization_barrier(jnp.sum(exp_cached, axis=-1, keepdims=True)) + lax.optimization_barrier(jnp.sum(exp_fresh, axis=-1, keepdims=True))
    weight_cached = (exp_cached / denominator).astype(jnp.bfloat16).astype(jnp.float32)
    weight_fresh = (exp_fresh / denominator).astype(jnp.bfloat16).astype(jnp.float32)
    combined = jnp.einsum('rkgsl,rlkd->rskgd', weight_cached, cache_values) + jnp.einsum('rkgst,rtkd->rskgd', weight_fresh, new_values)
    return combined.reshape(req_count, step_count, QUERY_HEADS * HEAD_WIDTH).astype(jnp.bfloat16)

def reference(hidden_input, query_matrix, adapter_down_weight, adapter_up_weight, request_adapter, adapter_slot, cached_key_value, fresh_key_value, cached_length):
    base_query = jnp.dot(hidden_input.reshape(REQS * STEPS, MODEL_WIDTH), query_matrix, preferred_element_type=jnp.float32)
    base_query = base_query.reshape(REQS, STEPS, QUERY_HEADS * HEAD_WIDTH)
    slot_ids = adapter_slot[request_adapter].astype(jnp.int32)

    def per_request(request_item):
        request_rows, pool_slot_index = request_item
        down_row_block = lax.dynamic_index_in_dim(adapter_down_weight, pool_slot_index, 0, keepdims=False)
        up_row_block = lax.dynamic_index_in_dim(adapter_up_weight, pool_slot_index, 0, keepdims=False)
        low_rows = lax.dot_general(request_rows, down_row_block, (((1,), (1,)), ((), ())), preferred_element_type=jnp.float32)
        low_rows = low_rows.astype(jnp.bfloat16)
        return jnp.dot(low_rows, up_row_block, preferred_element_type=jnp.float32)
    low_delta = lax.map(per_request, (hidden_input, slot_ids))
    queries = (base_query + low_delta).astype(jnp.bfloat16)
    return attend(queries, cached_key_value, fresh_key_value, cached_length)
```

```python
import functools
import math
from typing import NamedTuple

import jax
import jax.numpy as jnp
from jax import lax
from jax.experimental import pallas as pl
from jax.experimental.pallas import tpu as pltpu
from jax.sharding import PartitionSpec as P

QUERY_HEADS = 32
KVH = 4
HEAD_WIDTH = 128
CHUNKS = 2
LINK = jnp.float32
LINK_SCALE = 1.0
MESH = pl.DeviceIdType.MESH


def attend(queries, cached_key_value, fresh_key_value, cached_length):
    req_count = queries.shape[0]
    step_count = queries.shape[1]
    cache_size = cached_key_value.shape[2]
    group_size = QUERY_HEADS // KVH
    head_rows = queries.reshape(req_count, step_count, KVH, group_size, HEAD_WIDTH)
    cache_keys = cached_key_value[:, 0].reshape(req_count, cache_size, KVH, HEAD_WIDTH)
    cache_values = cached_key_value[:, 1].reshape(req_count, cache_size, KVH, HEAD_WIDTH)
    new_keys = fresh_key_value[:, 0].reshape(req_count, step_count, KVH, HEAD_WIDTH)
    new_values = fresh_key_value[:, 1].reshape(req_count, step_count, KVH, HEAD_WIDTH)
    score_scale = 1.0 / math.sqrt(HEAD_WIDTH)
    cached_scores = (
        jnp.einsum("rskgd,rlkd->rkgsl", head_rows, cache_keys, preferred_element_type=jnp.float32)
        * score_scale
    )
    fresh_scores = (
        jnp.einsum("rskgd,rtkd->rkgst", head_rows, new_keys, preferred_element_type=jnp.float32)
        * score_scale
    )
    valid_old = (jnp.arange(cache_size, dtype=jnp.int32)[None, :] < cached_length[:, None])[
        :, None, None, None, :
    ]
    valid_new = (
        jnp.arange(step_count, dtype=jnp.int32)[None, :]
        <= jnp.arange(step_count, dtype=jnp.int32)[:, None]
    )[None, None, None]
    cached_scores = jnp.where(valid_old, cached_scores, -1e30)
    fresh_scores = jnp.where(valid_new, fresh_scores, -1e30)
    row_max = jnp.maximum(jnp.max(cached_scores, axis=-1), jnp.max(fresh_scores, axis=-1))[
        ..., None
    ]
    exp_cached = jnp.exp(cached_scores - row_max)
    exp_fresh = jnp.exp(fresh_scores - row_max)
    denominator = jnp.sum(exp_cached, axis=-1, keepdims=True) + jnp.sum(
        exp_fresh, axis=-1, keepdims=True
    )
    weight_cached = (exp_cached / denominator).astype(jnp.bfloat16)
    weight_fresh = (exp_fresh / denominator).astype(jnp.bfloat16)
    combined = jnp.einsum(
        "rkgsl,rlkd->rskgd", weight_cached, cache_values, preferred_element_type=jnp.float32
    )
    combined = combined + jnp.einsum(
        "rkgst,rtkd->rskgd", weight_fresh, new_values, preferred_element_type=jnp.float32
    )
    return combined.reshape(req_count, step_count, QUERY_HEADS * HEAD_WIDTH).astype(jnp.bfloat16)


def per_device(
    hidden_input,
    query_matrix,
    adapter_down_weight,
    adapter_up_weight,
    request_adapter,
    adapter_slot,
    cached_key_value,
    fresh_key_value,
    cached_length,
):
    req_dev = hidden_input.shape[0]
    step_count = hidden_input.shape[1]
    width_of_model = hidden_input.shape[2]
    tensor_count = lax.axis_size("tensor")
    n_pool = lax.axis_size("pool")
    tensor_idx = lax.axis_index("tensor")
    pool_idx = lax.axis_index("pool")
    slots_per_device = adapter_up_weight.shape[0]
    adapter_rank_size = adapter_up_weight.shape[1]
    head_column_block = query_matrix.shape[1]
    group_rows = tensor_count * req_dev * step_count
    gathered, group_ids = (
        lax.all_gather(hidden_input, ("tensor", "pool"), axis=0, tiled=True),
        lax.all_gather(request_adapter, ("tensor", "pool"), axis=0, tiled=True),
    )
    adapters = adapter_slot.shape[0]
    id_match = group_ids[:, None] == jnp.arange(adapters, dtype=jnp.int32)[None, :]
    row_slot = jnp.sum(jnp.where(id_match, adapter_slot[None, :], 0), axis=1)
    owner_index = tensor_idx * n_pool + pool_idx
    own_slots = owner_index * slots_per_device + jnp.arange(slots_per_device, dtype=jnp.int32)
    own_mask = (row_slot[:, None] == own_slots[None, :]).astype(jnp.float32)
    flat_rows = gathered.reshape(-1, width_of_model)
    down_flattened = adapter_down_weight.reshape(
        slots_per_device * adapter_rank_size, width_of_model
    )
    projected = lax.dot_general(
        flat_rows, down_flattened, (((1,), (1,)), ((), ())), preferred_element_type=jnp.float32
    )
    masked = (
        projected.reshape(-1, step_count, slots_per_device, adapter_rank_size)
        * own_mask[:, None, :, None]
    )
    base_rows = gathered.reshape(tensor_count, n_pool, req_dev * step_count, width_of_model)
    own_group = lax.dynamic_index_in_dim(base_rows, pool_idx, 1, keepdims=False).reshape(
        group_rows, width_of_model
    )
    base_query = jnp.dot(own_group, query_matrix, preferred_element_type=jnp.float32)
    low_rows = masked.astype(jnp.bfloat16).reshape(
        tensor_count, n_pool, req_dev * step_count, slots_per_device * adapter_rank_size
    )
    by_group = jnp.transpose(low_rows, (1, 0, 2, 3)).reshape(
        n_pool, group_rows, slots_per_device * adapter_rank_size
    )
    up_weight_blocks = adapter_up_weight.reshape(
        slots_per_device * adapter_rank_size, tensor_count, head_column_block
    )
    block_count = group_rows * lax.axis_size(("tensor", "pool")) // group_rows
    block_index = jnp.arange(block_count, dtype=jnp.int32)
    head_block = block_index // n_pool
    group_index = block_index % n_pool
    picked_rows = jnp.take(by_group, group_index, axis=0)
    picked_cols = jnp.take(up_weight_blocks, head_block, axis=1)
    partial_sum = jnp.einsum(
        "brk,kbc->brc", picked_rows, picked_cols, preferred_element_type=jnp.float32
    )
    low_delta = lax.psum_scatter(
        partial_sum.reshape(block_count * group_rows, head_column_block),
        ("tensor", "pool"),
        scatter_dimension=0,
        tiled=True,
    )
    queries = (base_query + low_delta).astype(jnp.bfloat16)
    regrouped = lax.all_to_all(
        queries.reshape(tensor_count, req_dev * step_count, head_column_block),
        "tensor",
        split_axis=0,
        concat_axis=2,
        tiled=True,
    )
    return attend(regrouped, cached_key_value, fresh_key_value, cached_length)

def fused(
    dims,
    hidden_ref, matrix_ref, down_ref, up_ref, adapter_ref, table_ref, cache_ref, fresh_ref, length_ref,
    out_ref,
    gath, matrix_v, down_v, up_v, cache_v, hidden_v, fresh_v, adapter_s, table_s, length_s, slots,
    exch_out, exch_in, delta_out, delta_in, base_out, base_in,
    load_sem, small_sem, z_send, z_recv, f_send, f_recv, s_send, s_recv,
    x_send, x_recv, d_send, d_recv, b_send, b_recv,
):
    T, NC = dims.tensor, dims.chunks
    R = 2 * T
    steps, width = hidden_ref.shape[1], hidden_ref.shape[2]
    rows = R * steps
    part = width // NC
    lanes = part // 4
    half = matrix_v.shape[1]
    span = half * 2
    slot_count, rank = down_ref.shape[0], down_ref.shape[1]
    kvw = cache_ref.shape[3]
    cache_size = cache_ref.shape[2]
    t = lax.axis_index("tensor")
    p = lax.axis_index("pool")
    other = 1 - p
    me = t * 2 + p

    def up_t(j):
        return lax.rem(t + j, T)

    def down_t(j):
        return lax.rem(t + T - j, T)

    def remote(src, dst, ssem, rsem, tt, pp):
        return pltpu.make_async_remote_copy(
            src_ref=src, dst_ref=dst, send_sem=ssem, recv_sem=rsem,
            device_id={"tensor": tt, "pool": pp}, device_id_type=MESH,
        )

    smalls = [
        pltpu.make_async_copy(src, dst, small_sem.at[n])
        for n, (src, dst) in enumerate(
            (
                (hidden_ref.at[0], hidden_v),
                (adapter_ref, adapter_s),
                (table_ref, table_s),
                (fresh_ref.at[0], fresh_v),
                (length_ref, length_s),
            )
        )
    ]
    for load in smalls:
        load.start()
    mat_cols = pl.ds(pl.multiple_of(p * half, half), half)
    mat_loads, down_loads = [], []
    for c in range(NC):
        ks = pl.ds(c * part, part)
        mat_loads.append(pltpu.make_async_copy(matrix_ref.at[ks, mat_cols], matrix_v.at[ks], load_sem.at[2 * c]))
        down_loads.append(pltpu.make_async_copy(down_ref.at[:, :, ks], down_v.at[:, :, ks], load_sem.at[2 * c + 1]))
        mat_loads[c].start()
        down_loads[c].start()
    up_load = pltpu.make_async_copy(up_ref, up_v, load_sem.at[2 * NC])
    cache_load = pltpu.make_async_copy(cache_ref.at[0], cache_v, load_sem.at[2 * NC + 1])
    up_load.start()
    cache_load.start()

    barrier = pltpu.get_barrier_semaphore()
    for j in range(T):
        for q in range(2):
            if j or q:
                pl.semaphore_signal(
                    barrier, inc=1, device_id={"tensor": up_t(j), "pool": other if q else p}, device_id_type=MESH
                )

    smalls[0].wait()
    own = hidden_v[...].astype(jnp.float32)
    for c in range(NC):
        pieces = [own[:, c * part + q * lanes : c * part + (q + 1) * lanes] for q in range(4)]
        gath[c, 0] = jnp.concatenate(pieces, axis=0).astype(jnp.bfloat16)
    smalls[1].wait()
    smalls[2].wait()
    slots[0] = jnp.full((8, 128), table_s[adapter_s[0]], jnp.int32)

    pl.semaphore_wait(barrier, R - 1)

    pending = []
    zc, fc = {}, {}
    for c in range(NC):
        for j in range(1, T):
            zc[c, j] = remote(gath.at[c, 0], gath.at[c, 2 * j], z_send.at[c, j], z_recv.at[c, j], up_t(j), p)
            zc[c, j].start()
            pending.append(zc[c, j])
        for j in range(T):
            fc[c, j] = remote(gath.at[c, 2 * j], gath.at[c, 2 * j + 1], f_send.at[c, j], f_recv.at[c, j], t, other)
            pending.append(fc[c, j])
        fc[c, 0].start()
    sc = []
    for r in range(1, R):
        s = remote(slots.at[0], slots.at[r], s_send.at[r], s_recv.at[r], up_t(r // 2), other if r % 2 else p)
        s.start()
        sc.append(s)
        pending.append(s)

    i0 = lax.broadcasted_iota(jnp.int32, (4 * rows, 4 * rows), 0)
    i1 = lax.broadcasted_iota(jnp.int32, (4 * rows, 4 * rows), 1)
    q0 = lax.div(i0, rows)
    r0 = lax.div(lax.rem(i0, rows), steps)
    s0 = lax.rem(i0, steps)
    order = jnp.where(i1 == r0 * (4 * steps) + q0 * steps + s0, 1.0, 0.0).astype(jnp.bfloat16)

    smalls[3].wait()
    smalls[4].wait()
    fresh = fresh_v[...].astype(jnp.float32)
    pad = jnp.zeros((128 - steps, kvw), jnp.float32)
    fresh_keys = jnp.concatenate([fresh[0], pad], axis=0).astype(jnp.bfloat16)
    fresh_vals = jnp.concatenate([fresh[1], pad], axis=0).astype(jnp.bfloat16)

    base = jnp.zeros((rows, half), jnp.float32)
    low_t = jnp.zeros((slot_count * rank, rows), jnp.float32)
    for c in range(NC):
        for j in range(1, T):
            zc[c, j].wait_recv()
            fc[c, j].start()
        for j in range(T):
            fc[c, j].wait_recv()
        mat_loads[c].wait()
        down_loads[c].wait()
        arrived = gath[c].reshape(R * 4 * steps, lanes)
        ordered = jnp.dot(order, arrived, preferred_element_type=jnp.float32).astype(jnp.bfloat16)
        for q in range(4):
            lhs = ordered[q * rows : (q + 1) * rows]
            k0 = c * part + q * lanes
            dn = down_v[:, :, k0 : k0 + lanes].reshape(slot_count * rank, lanes)
            low_t += lax.dot_general(dn, lhs, (((1,), (1,)), ((), ())), preferred_element_type=jnp.float32)
            base += jnp.dot(lhs, matrix_v[k0 : k0 + lanes, :], preferred_element_type=jnp.float32)

    h2 = half // 2
    bc = []
    for r in range(R):
        rb = base[r * steps : (r + 1) * steps]
        block = jnp.concatenate([rb[:, :h2], rb[:, h2:]], axis=0)
        if r == 0:
            base_in[me] = block
        else:
            base_out[r] = block
            tt, pp = down_t(r // 2), (other if r % 2 else p)
            b = remote(base_out.at[r], base_in.at[me], b_send.at[r], b_recv.at[r], tt, pp)
            b.start()
            bc.append(b)

    for s in sc:
        s.wait_recv()
    ri = lax.broadcasted_iota(jnp.int32, (rows, 128), 0)
    row_slot = jnp.zeros((rows, 128), jnp.int32)
    for r in range(R):
        here = (ri >= r * steps) & (ri < (r + 1) * steps)
        row_slot = jnp.where(here, jnp.broadcast_to(slots[r, 0:1, :], (rows, 128)), row_slot)
    low = low_t.T
    bits = []
    for n in range(slot_count * rank // 128):
        col_slot = me * slot_count + lax.div(lax.broadcasted_iota(jnp.int32, (rows, 128), 1) + n * 128, rank)
        bits.append(jnp.where(row_slot == col_slot, low[:, n * 128 : (n + 1) * 128], 0.0))
    low = jnp.concatenate(bits, axis=1).astype(jnp.bfloat16)

    up_load.wait()
    deltas = []
    for k in range(T):
        upk = up_v[:, :, k * span : (k + 1) * span].reshape(slot_count * rank, span)
        deltas.append(jnp.dot(low, upk, preferred_element_type=jnp.float32))

    def block_of(r):
        return jnp.concatenate([d[r * steps : (r + 1) * steps] for d in deltas], axis=0)

    order_j = list(range(1, T)) + [0]
    xc, dc = {}, {}
    for j in order_j:
        exch_out[j] = (block_of(2 * j + 1) * LINK_SCALE).astype(LINK)
        xc[j] = remote(exch_out.at[j], exch_in.at[j], x_send.at[j], x_recv.at[j], t, other)
        xc[j].start()
        pending.append(xc[j])
    mine = {j: block_of(2 * j) for j in order_j}
    for j in order_j:
        xc[j].wait_recv()
        both = mine[j] * LINK_SCALE + exch_in[j].astype(jnp.float32)
        if j:
            delta_out[j] = both.astype(LINK)
            dc[j] = remote(delta_out.at[j], delta_in.at[j], d_send.at[j], d_recv.at[j], down_t(j), p)
            dc[j].start()
            pending.append(dc[j])
        else:
            total = both

    cache_load.wait()
    for b in bc:
        b.wait_recv()
    parts = []
    for tt in range(T):
        pieces = []
        for pp in range(2):
            got = base_in[tt * 2 + pp]
            pieces += [got[:steps], got[steps:]]
        parts.append(jnp.concatenate(pieces, axis=1))
    base_rows = jnp.concatenate(parts, axis=0)
    for j in range(1, T):
        dc[j].wait_recv()
        total = total + delta_in[j].astype(jnp.float32)
    queries = (base_rows + total * (1.0 / LINK_SCALE)).astype(jnp.bfloat16).astype(jnp.float32)

    groups = span // HEAD_WIDTH
    heads = groups * steps
    scale = 1.0 / math.sqrt(HEAD_WIDTH)
    length = length_s[0]
    old_ok = lax.broadcasted_iota(jnp.int32, (heads, cache_size), 1) < length
    step_of = lax.rem(lax.broadcasted_iota(jnp.int32, (heads, 128), 0), steps)
    new_ok = lax.broadcasted_iota(jnp.int32, (heads, 128), 1) <= step_of
    nt = (((1,), (1,)), ((), ()))
    for k in range(T):
        rows_k = queries[k * steps : (k + 1) * steps]
        qk = jnp.concatenate(
            [rows_k[:, g * HEAD_WIDTH : (g + 1) * HEAD_WIDTH] for g in range(groups)], axis=0
        ).astype(jnp.bfloat16)
        cols = slice(k * HEAD_WIDTH, (k + 1) * HEAD_WIDTH)
        old = lax.dot_general(qk, cache_v[0, :, cols], nt, preferred_element_type=jnp.float32) * scale
        new = lax.dot_general(qk, fresh_keys[:, cols], nt, preferred_element_type=jnp.float32) * scale
        old = jnp.where(old_ok, old, -1e30)
        new = jnp.where(new_ok, new, -1e30)
        top = jnp.maximum(jnp.max(old, axis=1, keepdims=True), jnp.max(new, axis=1, keepdims=True))
        old = jnp.exp(old - top)
        new = jnp.exp(new - top)
        den = jnp.sum(old, axis=1, keepdims=True) + jnp.sum(new, axis=1, keepdims=True)
        inv = 1.0 / den
        res = jnp.dot((old * inv).astype(jnp.bfloat16), cache_v[1, :, cols], preferred_element_type=jnp.float32)
        res += jnp.dot((new * inv).astype(jnp.bfloat16), fresh_vals[:, cols], preferred_element_type=jnp.float32)
        flat = jnp.concatenate([res[g * steps : (g + 1) * steps] for g in range(groups)], axis=1)
        out_ref[0, :, k * span : (k + 1) * span] = flat.astype(jnp.bfloat16)

    for x in pending + bc:
        x.wait_send()


class Dims(NamedTuple):
    tensor: int
    chunks: int


def fused_call(
    hidden_input, query_matrix, adapter_down_weight, adapter_up_weight,
    request_adapter, adapter_slot, cached_key_value, fresh_key_value, cached_length,
):
    T = lax.axis_size("tensor")
    NC = CHUNKS
    R = 2 * T
    steps, width = hidden_input.shape[1], hidden_input.shape[2]
    lanes = width // NC // 4
    half = query_matrix.shape[1] // 2
    span = half * 2
    bf, f32 = jnp.bfloat16, jnp.float32
    V, S = pltpu.VMEM, pltpu.SemaphoreType.DMA
    vm, hb = (pl.BlockSpec(memory_space=m) for m in (pltpu.VMEM, pl.ANY))
    M = pltpu.SMEM
    return pl.pallas_call(
        functools.partial(fused, Dims(T, NC)),
        out_shape=jax.ShapeDtypeStruct((1, steps, span * T), bf),
        in_specs=[hb] * 9,
        out_specs=vm,
        scratch_shapes=[
            V((NC, R, 4 * steps, lanes), bf),
            V((width, half), bf),
            V(adapter_down_weight.shape, bf),
            V(adapter_up_weight.shape, bf),
            V(cached_key_value.shape[1:], bf),
            V(hidden_input.shape[1:], bf),
            V(fresh_key_value.shape[1:], bf),
            M((1,), jnp.int32),
            M(adapter_slot.shape, jnp.int32),
            M((1,), jnp.int32),
            V((R, 8, 128), jnp.int32),
            V((T, T * steps, span), LINK),
            V((T, T * steps, span), LINK),
            V((T, T * steps, span), LINK),
            V((T, T * steps, span), LINK),
            V((R, 2 * steps, half // 2), f32),
            V((R, 2 * steps, half // 2), f32),
            S((2 * NC + 2,)),
            S((5,)),
            S((NC, T)), S((NC, T)), S((NC, T)), S((NC, T)),
            S((R,)), S((R,)),
            S((T,)), S((T,)), S((T,)), S((T,)),
            S((R,)), S((R,)),
        ],
        compiler_params=pltpu.CompilerParams(
            collective_id=0, has_side_effects=True, vmem_limit_bytes=62 * 1024 * 1024
        ),
        cost_estimate=pl.CostEstimate(flops=10**9, bytes_accessed=16 * 10**6, transcendentals=10**5),
    )(
        hidden_input, query_matrix, adapter_down_weight, adapter_up_weight,
        request_adapter, adapter_slot, cached_key_value, fresh_key_value, cached_length,
    )


def fits_fused(hidden, matrix, down, cache):
    return (
        lax.axis_size("tensor") == KVH
        and lax.axis_size("pool") == 2
        and hidden.shape[0] == 1
        and hidden.shape[1] == 4
        and matrix.shape[1] == QUERY_HEADS // KVH * HEAD_WIDTH
        and (down.shape[0] * down.shape[1]) % 128 == 0
        and hidden.shape[2] % (CHUNKS * 4 * 128) == 0
        and cache.shape[2] % 128 == 0
    )

def either(*arrays):
    hidden, matrix, down, cache = arrays[0], arrays[1], arrays[2], arrays[6]
    if fits_fused(hidden, matrix, down, cache):
        return fused_call(*arrays)
    return per_device(*arrays)


def solution(mesh):
    placed = (
        P(("groups", "tensor", "batch", "pool"), None, None),
        P(None, "tensor"),
        P(("tensor", "pool"), None, None),
        P(("tensor", "pool"), None, None),
        P(("groups", "tensor", "batch", "pool")),
        P(),
        P(("groups", "tensor", "batch", "pool"), None, None, None),
        P(("groups", "tensor", "batch", "pool"), None, None, None),
        P(("groups", "tensor", "batch", "pool")),
    )
    return jax.shard_map(
        either,
        mesh=mesh,
        in_specs=placed,
        out_specs=P(("groups", "tensor", "batch", "pool"), None, None),
        check_vma=False,
    )
```

```python
import functools
import math
from typing import NamedTuple

import jax
import jax.numpy as jnp
from jax import lax
from jax.experimental import pallas as pl
from jax.experimental.pallas import tpu as pltpu
from jax.sharding import PartitionSpec as P

QUERY_HEADS = 32
KVH = 4
HEAD_WIDTH = 128
CHUNKS = 2
LINK = jnp.float32
MESH = pl.DeviceIdType.MESH


def attend(queries, cached_key_value, fresh_key_value, cached_length):
    req_count = queries.shape[0]
    step_count = queries.shape[1]
    cache_size = cached_key_value.shape[2]
    group_size = QUERY_HEADS // KVH
    head_rows = queries.reshape(req_count, step_count, KVH, group_size, HEAD_WIDTH)
    cache_keys = cached_key_value[:, 0].reshape(req_count, cache_size, KVH, HEAD_WIDTH)
    cache_values = cached_key_value[:, 1].reshape(req_count, cache_size, KVH, HEAD_WIDTH)
    new_keys = fresh_key_value[:, 0].reshape(req_count, step_count, KVH, HEAD_WIDTH)
    new_values = fresh_key_value[:, 1].reshape(req_count, step_count, KVH, HEAD_WIDTH)
    score_scale = 1.0 / math.sqrt(HEAD_WIDTH)
    cached_scores = (
        jnp.einsum("rskgd,rlkd->rkgsl", head_rows, cache_keys, preferred_element_type=jnp.float32)
        * score_scale
    )
    fresh_scores = (
        jnp.einsum("rskgd,rtkd->rkgst", head_rows, new_keys, preferred_element_type=jnp.float32)
        * score_scale
    )
    valid_old = (jnp.arange(cache_size, dtype=jnp.int32)[None, :] < cached_length[:, None])[
        :, None, None, None, :
    ]
    valid_new = (
        jnp.arange(step_count, dtype=jnp.int32)[None, :]
        <= jnp.arange(step_count, dtype=jnp.int32)[:, None]
    )[None, None, None]
    cached_scores = jnp.where(valid_old, cached_scores, -1e30)
    fresh_scores = jnp.where(valid_new, fresh_scores, -1e30)
    row_max = jnp.maximum(jnp.max(cached_scores, axis=-1), jnp.max(fresh_scores, axis=-1))[
        ..., None
    ]
    exp_cached = jnp.exp(cached_scores - row_max)
    exp_fresh = jnp.exp(fresh_scores - row_max)
    denominator = jnp.sum(exp_cached, axis=-1, keepdims=True) + jnp.sum(
        exp_fresh, axis=-1, keepdims=True
    )
    weight_cached = (exp_cached / denominator).astype(jnp.bfloat16)
    weight_fresh = (exp_fresh / denominator).astype(jnp.bfloat16)
    combined = jnp.einsum(
        "rkgsl,rlkd->rskgd", weight_cached, cache_values, preferred_element_type=jnp.float32
    )
    combined = combined + jnp.einsum(
        "rkgst,rtkd->rskgd", weight_fresh, new_values, preferred_element_type=jnp.float32
    )
    return combined.reshape(req_count, step_count, QUERY_HEADS * HEAD_WIDTH).astype(jnp.bfloat16)


def per_device(
    hidden_input,
    query_matrix,
    adapter_down_weight,
    adapter_up_weight,
    request_adapter,
    adapter_slot,
    cached_key_value,
    fresh_key_value,
    cached_length,
):
    req_dev = hidden_input.shape[0]
    step_count = hidden_input.shape[1]
    width_of_model = hidden_input.shape[2]
    tensor_count = lax.axis_size("tensor")
    n_pool = lax.axis_size("pool")
    tensor_idx = lax.axis_index("tensor")
    pool_idx = lax.axis_index("pool")
    slots_per_device = adapter_up_weight.shape[0]
    adapter_rank_size = adapter_up_weight.shape[1]
    head_column_block = query_matrix.shape[1]
    group_rows = tensor_count * req_dev * step_count
    gathered, group_ids = (
        lax.all_gather(hidden_input, ("tensor", "pool"), axis=0, tiled=True),
        lax.all_gather(request_adapter, ("tensor", "pool"), axis=0, tiled=True),
    )
    adapters = adapter_slot.shape[0]
    id_match = group_ids[:, None] == jnp.arange(adapters, dtype=jnp.int32)[None, :]
    row_slot = jnp.sum(jnp.where(id_match, adapter_slot[None, :], 0), axis=1)
    owner_index = tensor_idx * n_pool + pool_idx
    own_slots = owner_index * slots_per_device + jnp.arange(slots_per_device, dtype=jnp.int32)
    own_mask = (row_slot[:, None] == own_slots[None, :]).astype(jnp.float32)
    flat_rows = gathered.reshape(-1, width_of_model)
    down_flattened = adapter_down_weight.reshape(
        slots_per_device * adapter_rank_size, width_of_model
    )
    projected = lax.dot_general(
        flat_rows, down_flattened, (((1,), (1,)), ((), ())), preferred_element_type=jnp.float32
    )
    masked = (
        projected.reshape(-1, step_count, slots_per_device, adapter_rank_size)
        * own_mask[:, None, :, None]
    )
    base_rows = gathered.reshape(tensor_count, n_pool, req_dev * step_count, width_of_model)
    own_group = lax.dynamic_index_in_dim(base_rows, pool_idx, 1, keepdims=False).reshape(
        group_rows, width_of_model
    )
    base_query = jnp.dot(own_group, query_matrix, preferred_element_type=jnp.float32)
    low_rows = masked.astype(jnp.bfloat16).reshape(
        tensor_count, n_pool, req_dev * step_count, slots_per_device * adapter_rank_size
    )
    by_group = jnp.transpose(low_rows, (1, 0, 2, 3)).reshape(
        n_pool, group_rows, slots_per_device * adapter_rank_size
    )
    up_weight_blocks = adapter_up_weight.reshape(
        slots_per_device * adapter_rank_size, tensor_count, head_column_block
    )
    block_count = group_rows * lax.axis_size(("tensor", "pool")) // group_rows
    block_index = jnp.arange(block_count, dtype=jnp.int32)
    head_block = block_index // n_pool
    group_index = block_index % n_pool
    picked_rows = jnp.take(by_group, group_index, axis=0)
    picked_cols = jnp.take(up_weight_blocks, head_block, axis=1)
    partial_sum = jnp.einsum(
        "brk,kbc->brc", picked_rows, picked_cols, preferred_element_type=jnp.float32
    )
    low_delta = lax.psum_scatter(
        partial_sum.reshape(block_count * group_rows, head_column_block),
        ("tensor", "pool"),
        scatter_dimension=0,
        tiled=True,
    )
    queries = (base_query + low_delta).astype(jnp.bfloat16)
    regrouped = lax.all_to_all(
        queries.reshape(tensor_count, req_dev * step_count, head_column_block),
        "tensor",
        split_axis=0,
        concat_axis=2,
        tiled=True,
    )
    return attend(regrouped, cached_key_value, fresh_key_value, cached_length)

def fused(
    dims,
    hidden_ref, matrix_ref, down_ref, up_ref, adapter_ref, table_ref, cache_ref, fresh_ref, length_ref,
    out_ref,
    gath, matrix_v, down_v, up_v, cache_v, hidden_v, fresh_v, adapter_s, table_s, length_s,
    exch_out, exch_in, delta_out, delta_in,
    load_sem, small_sem, z_send, z_recv, f_send, f_recv,
    x_send, x_recv, d_send, d_recv,
):
    T, NC = dims.tensor, dims.chunks
    R = 2 * T
    steps, width = hidden_ref.shape[1], hidden_ref.shape[2]
    rows = R * steps
    part = width // NC
    lanes = part // 4
    half = matrix_v.shape[1]
    span = half * 2
    slot_count, rank = down_ref.shape[0], down_ref.shape[1]
    kvw = cache_ref.shape[3]
    cache_size = cache_ref.shape[2]
    t = lax.axis_index("tensor")
    p = lax.axis_index("pool")
    other = 1 - p
    me = t * 2 + p

    def up_t(j):
        return lax.rem(t + j, T)

    def down_t(j):
        return lax.rem(t + T - j, T)

    def remote(src, dst, ssem, rsem, tt, pp):
        return pltpu.make_async_remote_copy(
            src_ref=src, dst_ref=dst, send_sem=ssem, recv_sem=rsem,
            device_id={"tensor": tt, "pool": pp}, device_id_type=MESH,
        )

    smalls = [
        pltpu.make_async_copy(src, dst, small_sem.at[n])
        for n, (src, dst) in enumerate(
            (
                (hidden_ref.at[0], hidden_v),
                (adapter_ref, adapter_s),
                (table_ref, table_s),
                (fresh_ref.at[0], fresh_v),
                (length_ref, length_s),
            )
        )
    ]
    for load in smalls:
        load.start()
    mat_cols = pl.ds(pl.multiple_of(p * half, half), half)
    mat_loads, down_loads = [], []
    for c in range(NC):
        ks = pl.ds(c * part, part)
        mat_loads.append(pltpu.make_async_copy(matrix_ref.at[ks, mat_cols], matrix_v.at[ks], load_sem.at[2 * c]))
        down_loads.append(pltpu.make_async_copy(down_ref.at[:, :, ks], down_v.at[:, :, ks], load_sem.at[2 * c + 1]))
        mat_loads[c].start()
        down_loads[c].start()
    up_load = pltpu.make_async_copy(up_ref, up_v, load_sem.at[2 * NC])
    cache_load = pltpu.make_async_copy(cache_ref.at[0], cache_v, load_sem.at[2 * NC + 1])
    up_load.start()
    cache_load.start()

    barrier = pltpu.get_barrier_semaphore()
    for j in range(T):
        for q in range(2):
            if j or q:
                pl.semaphore_signal(
                    barrier, inc=1, device_id={"tensor": up_t(j), "pool": other if q else p}, device_id_type=MESH
                )

    smalls[0].wait()
    own = hidden_v[...].astype(jnp.float32)
    for c in range(NC):
        pieces = [own[:, c * part + q * lanes : c * part + (q + 1) * lanes] for q in range(4)]
        gath[c, 0, :, :lanes] = jnp.concatenate(pieces, axis=0).astype(jnp.bfloat16)
    smalls[1].wait()
    smalls[2].wait()
    slot_block = jnp.full((4 * steps, 128), table_s[adapter_s[0]], jnp.int32).astype(jnp.float32).astype(jnp.bfloat16)
    for c in range(NC):
        gath[c, 0, :, lanes:] = slot_block

    pl.semaphore_wait(barrier, R - 1)

    pending = []
    zc, fc = {}, {}
    for c in range(NC):
        for j in range(1, T):
            zc[c, j] = remote(gath.at[c, 0], gath.at[c, 2 * j], z_send.at[c, j], z_recv.at[c, j], up_t(j), p)
            zc[c, j].start()
            pending.append(zc[c, j])
        for j in range(T):
            fc[c, j] = remote(gath.at[c, 2 * j], gath.at[c, 2 * j + 1], f_send.at[c, j], f_recv.at[c, j], t, other)
            pending.append(fc[c, j])
        fc[c, 0].start()
    i0 = lax.broadcasted_iota(jnp.int32, (4 * rows, 4 * rows), 0)
    i1 = lax.broadcasted_iota(jnp.int32, (4 * rows, 4 * rows), 1)
    q0 = lax.div(i0, rows)
    r0 = lax.div(lax.rem(i0, rows), steps)
    s0 = lax.rem(i0, steps)
    order = jnp.where(i1 == r0 * (4 * steps) + q0 * steps + s0, 1.0, 0.0).astype(jnp.bfloat16)

    smalls[3].wait()
    smalls[4].wait()
    fresh = fresh_v[...].astype(jnp.float32)
    pad = jnp.zeros((128 - steps, kvw), jnp.float32)
    fresh_keys = jnp.concatenate([fresh[0], pad], axis=0).astype(jnp.bfloat16)
    fresh_vals = jnp.concatenate([fresh[1], pad], axis=0).astype(jnp.bfloat16)

    base = jnp.zeros((rows, half), jnp.float32)
    low_t = jnp.zeros((slot_count * rank, rows), jnp.float32)
    for c in range(NC):
        for j in range(1, T):
            zc[c, j].wait_recv()
            fc[c, j].start()
        for j in range(T):
            fc[c, j].wait_recv()
        mat_loads[c].wait()
        down_loads[c].wait()
        arrived = gath[c, :, :, :lanes].reshape(R * 4 * steps, lanes)
        ordered = jnp.dot(order, arrived, preferred_element_type=jnp.float32).astype(jnp.bfloat16)
        for q in range(4):
            lhs = ordered[q * rows : (q + 1) * rows]
            k0 = c * part + q * lanes
            dn = down_v[:, :, k0 : k0 + lanes].reshape(slot_count * rank, lanes)
            low_t += lax.dot_general(dn, lhs, (((1,), (1,)), ((), ())), preferred_element_type=jnp.float32)
            base += jnp.dot(lhs, matrix_v[k0 : k0 + lanes, :], preferred_element_type=jnp.float32)

    ri = lax.broadcasted_iota(jnp.int32, (rows, 128), 0)
    row_slot = jnp.zeros((rows, 128), jnp.float32)
    for r in range(R):
        here = (ri >= r * steps) & (ri < (r + 1) * steps)
        row_slot = jnp.where(here, jnp.broadcast_to(gath[0, r, :, lanes:].astype(jnp.float32)[0:1], (rows, 128)), row_slot)
    low = low_t.T
    bits = []
    for n in range(slot_count * rank // 128):
        col_slot = me * slot_count + lax.div(lax.broadcasted_iota(jnp.int32, (rows, 128), 1) + n * 128, rank)
        bits.append(jnp.where(row_slot == col_slot.astype(jnp.float32), low[:, n * 128 : (n + 1) * 128], 0.0))
    low = jnp.concatenate(bits, axis=1).astype(jnp.bfloat16)

    up_load.wait()
    base_wide = jnp.concatenate([jnp.where(p == 0, base, 0.0), jnp.where(p == 1, base, 0.0)], axis=1)
    deltas = []
    for k in range(T):
        upk = up_v[:, :, k * span : (k + 1) * span].reshape(slot_count * rank, span)
        delta = jnp.dot(low, upk, preferred_element_type=jnp.float32)
        deltas.append(delta + jnp.where(t == k, base_wide, 0.0))

    def block_of(r):
        return jnp.concatenate([d[r * steps : (r + 1) * steps] for d in deltas], axis=0)

    order_j = list(range(1, T)) + [0]
    xc, dc = {}, {}
    for j in order_j:
        exch_out[j] = (block_of(2 * j + 1)).astype(LINK)
        xc[j] = remote(exch_out.at[j], exch_in.at[j], x_send.at[j], x_recv.at[j], t, other)
        xc[j].start()
        pending.append(xc[j])
    mine = {j: block_of(2 * j) for j in order_j}
    for j in order_j:
        xc[j].wait_recv()
        both = mine[j] + exch_in[j].astype(jnp.float32)
        if j:
            delta_out[j] = both.astype(LINK)
            dc[j] = remote(delta_out.at[j], delta_in.at[j], d_send.at[j], d_recv.at[j], down_t(j), p)
            dc[j].start()
            pending.append(dc[j])
        else:
            total = both

    cache_load.wait()
    for j in range(1, T):
        dc[j].wait_recv()
        total = total + delta_in[j].astype(jnp.float32)
    queries = total.astype(jnp.bfloat16).astype(jnp.float32)

    groups = span // HEAD_WIDTH
    heads = groups * steps
    scale = 1.0 / math.sqrt(HEAD_WIDTH)
    length = length_s[0]
    old_ok = lax.broadcasted_iota(jnp.int32, (heads, cache_size), 1) < length
    step_of = lax.rem(lax.broadcasted_iota(jnp.int32, (heads, 128), 0), steps)
    new_ok = lax.broadcasted_iota(jnp.int32, (heads, 128), 1) <= step_of
    nt = (((1,), (1,)), ((), ()))
    for k in range(T):
        rows_k = queries[k * steps : (k + 1) * steps]
        qk = jnp.concatenate(
            [rows_k[:, g * HEAD_WIDTH : (g + 1) * HEAD_WIDTH] for g in range(groups)], axis=0
        ).astype(jnp.bfloat16)
        cols = slice(k * HEAD_WIDTH, (k + 1) * HEAD_WIDTH)
        old = lax.dot_general(qk, cache_v[0, :, cols], nt, preferred_element_type=jnp.float32) * scale
        new = lax.dot_general(qk, fresh_keys[:, cols], nt, preferred_element_type=jnp.float32) * scale
        old = jnp.where(old_ok, old, -1e30)
        new = jnp.where(new_ok, new, -1e30)
        top = jnp.maximum(jnp.max(old, axis=1, keepdims=True), jnp.max(new, axis=1, keepdims=True))
        old = jnp.exp(old - top)
        new = jnp.exp(new - top)
        den = jnp.sum(old, axis=1, keepdims=True) + jnp.sum(new, axis=1, keepdims=True)
        inv = 1.0 / den
        res = jnp.dot((old * inv).astype(jnp.bfloat16), cache_v[1, :, cols], preferred_element_type=jnp.float32)
        res += jnp.dot((new * inv).astype(jnp.bfloat16), fresh_vals[:, cols], preferred_element_type=jnp.float32)
        flat = jnp.concatenate([res[g * steps : (g + 1) * steps] for g in range(groups)], axis=1)
        out_ref[0, :, k * span : (k + 1) * span] = flat.astype(jnp.bfloat16)

    for x in pending:
        x.wait_send()


class Dims(NamedTuple):
    tensor: int
    chunks: int


def fused_call(
    hidden_input, query_matrix, adapter_down_weight, adapter_up_weight,
    request_adapter, adapter_slot, cached_key_value, fresh_key_value, cached_length,
):
    T = lax.axis_size("tensor")
    NC = CHUNKS
    R = 2 * T
    steps, width = hidden_input.shape[1], hidden_input.shape[2]
    lanes = width // NC // 4
    half = query_matrix.shape[1] // 2
    span = half * 2
    bf, f32 = jnp.bfloat16, jnp.float32
    V, S = pltpu.VMEM, pltpu.SemaphoreType.DMA
    vm, hb = (pl.BlockSpec(memory_space=m) for m in (pltpu.VMEM, pl.ANY))
    M = pltpu.SMEM
    return pl.pallas_call(
        functools.partial(fused, Dims(T, NC)),
        out_shape=jax.ShapeDtypeStruct((1, steps, span * T), bf),
        in_specs=[hb] * 9,
        out_specs=vm,
        scratch_shapes=[
            V((NC, R, 4 * steps, lanes + 128), bf),
            V((width, half), bf),
            V(adapter_down_weight.shape, bf),
            V(adapter_up_weight.shape, bf),
            V(cached_key_value.shape[1:], bf),
            V(hidden_input.shape[1:], bf),
            V(fresh_key_value.shape[1:], bf),
            M((1,), jnp.int32),
            M(adapter_slot.shape, jnp.int32),
            M((1,), jnp.int32),
            V((T, T * steps, span), LINK),
            V((T, T * steps, span), LINK),
            V((T, T * steps, span), LINK),
            V((T, T * steps, span), LINK),
            S((2 * NC + 2,)),
            S((5,)),
            S((NC, T)), S((NC, T)), S((NC, T)), S((NC, T)),
            S((T,)), S((T,)), S((T,)), S((T,)),
        ],
        compiler_params=pltpu.CompilerParams(
            collective_id=0, has_side_effects=True, vmem_limit_bytes=62 * 1024 * 1024
        ),
        cost_estimate=pl.CostEstimate(flops=10**9, bytes_accessed=16 * 10**6, transcendentals=10**5),
    )(
        hidden_input, query_matrix, adapter_down_weight, adapter_up_weight,
        request_adapter, adapter_slot, cached_key_value, fresh_key_value, cached_length,
    )


def fits_fused(hidden, matrix, down, cache):
    return (
        lax.axis_size("tensor") == KVH
        and lax.axis_size("pool") == 2
        and hidden.shape[0] == 1
        and hidden.shape[1] == 4
        and matrix.shape[1] == QUERY_HEADS // KVH * HEAD_WIDTH
        and (down.shape[0] * down.shape[1]) % 128 == 0
        and down.shape[0] * 2 * KVH <= 256
        and hidden.shape[2] % (CHUNKS * 4 * 128) == 0
        and cache.shape[2] % 128 == 0
    )

def either(*arrays):
    hidden, matrix, down, cache = arrays[0], arrays[1], arrays[2], arrays[6]
    if fits_fused(hidden, matrix, down, cache):
        return fused_call(*arrays)
    return per_device(*arrays)


def solution(mesh):
    placed = (
        P(("groups", "tensor", "batch", "pool"), None, None),
        P(None, "tensor"),
        P(("tensor", "pool"), None, None),
        P(("tensor", "pool"), None, None),
        P(("groups", "tensor", "batch", "pool")),
        P(),
        P(("groups", "tensor", "batch", "pool"), None, None, None),
        P(("groups", "tensor", "batch", "pool"), None, None, None),
        P(("groups", "tensor", "batch", "pool")),
    )
    return jax.shard_map(
        either,
        mesh=mesh,
        in_specs=placed,
        out_specs=P(("groups", "tensor", "batch", "pool"), None, None),
        check_vma=False,
    )
```

```python
import functools
import math
from typing import NamedTuple

import jax
import jax.numpy as jnp
from jax import lax
from jax.experimental import pallas as pl
from jax.experimental.pallas import tpu as pltpu
from jax.sharding import PartitionSpec as P

QUERY_HEADS = 32
KVH = 4
HEAD_WIDTH = 128
CHUNKS = 2
LINK = jnp.float32
MESH = pl.DeviceIdType.MESH


def attend(queries, cached_key_value, fresh_key_value, cached_length):
    req_count = queries.shape[0]
    step_count = queries.shape[1]
    cache_size = cached_key_value.shape[2]
    group_size = QUERY_HEADS // KVH
    head_rows = queries.reshape(req_count, step_count, KVH, group_size, HEAD_WIDTH)
    cache_keys = cached_key_value[:, 0].reshape(req_count, cache_size, KVH, HEAD_WIDTH)
    cache_values = cached_key_value[:, 1].reshape(req_count, cache_size, KVH, HEAD_WIDTH)
    new_keys = fresh_key_value[:, 0].reshape(req_count, step_count, KVH, HEAD_WIDTH)
    new_values = fresh_key_value[:, 1].reshape(req_count, step_count, KVH, HEAD_WIDTH)
    score_scale = 1.0 / math.sqrt(HEAD_WIDTH)
    cached_scores = (
        jnp.einsum("rskgd,rlkd->rkgsl", head_rows, cache_keys, preferred_element_type=jnp.float32)
        * score_scale
    )
    fresh_scores = (
        jnp.einsum("rskgd,rtkd->rkgst", head_rows, new_keys, preferred_element_type=jnp.float32)
        * score_scale
    )
    valid_old = (jnp.arange(cache_size, dtype=jnp.int32)[None, :] < cached_length[:, None])[
        :, None, None, None, :
    ]
    valid_new = (
        jnp.arange(step_count, dtype=jnp.int32)[None, :]
        <= jnp.arange(step_count, dtype=jnp.int32)[:, None]
    )[None, None, None]
    cached_scores = jnp.where(valid_old, cached_scores, -1e30)
    fresh_scores = jnp.where(valid_new, fresh_scores, -1e30)
    row_max = jnp.maximum(jnp.max(cached_scores, axis=-1), jnp.max(fresh_scores, axis=-1))[
        ..., None
    ]
    exp_cached = jnp.exp(cached_scores - row_max)
    exp_fresh = jnp.exp(fresh_scores - row_max)
    denominator = jnp.sum(exp_cached, axis=-1, keepdims=True) + jnp.sum(
        exp_fresh, axis=-1, keepdims=True
    )
    weight_cached = (exp_cached / denominator).astype(jnp.bfloat16)
    weight_fresh = (exp_fresh / denominator).astype(jnp.bfloat16)
    combined = jnp.einsum(
        "rkgsl,rlkd->rskgd", weight_cached, cache_values, preferred_element_type=jnp.float32
    )
    combined = combined + jnp.einsum(
        "rkgst,rtkd->rskgd", weight_fresh, new_values, preferred_element_type=jnp.float32
    )
    return combined.reshape(req_count, step_count, QUERY_HEADS * HEAD_WIDTH).astype(jnp.bfloat16)


def per_device(
    hidden_input,
    query_matrix,
    adapter_down_weight,
    adapter_up_weight,
    request_adapter,
    adapter_slot,
    cached_key_value,
    fresh_key_value,
    cached_length,
):
    req_dev = hidden_input.shape[0]
    step_count = hidden_input.shape[1]
    width_of_model = hidden_input.shape[2]
    tensor_count = lax.axis_size("tensor")
    n_pool = lax.axis_size("pool")
    tensor_idx = lax.axis_index("tensor")
    pool_idx = lax.axis_index("pool")
    slots_per_device = adapter_up_weight.shape[0]
    adapter_rank_size = adapter_up_weight.shape[1]
    head_column_block = query_matrix.shape[1]
    group_rows = tensor_count * req_dev * step_count
    gathered, group_ids = (
        lax.all_gather(hidden_input, ("tensor", "pool"), axis=0, tiled=True),
        lax.all_gather(request_adapter, ("tensor", "pool"), axis=0, tiled=True),
    )
    adapters = adapter_slot.shape[0]
    id_match = group_ids[:, None] == jnp.arange(adapters, dtype=jnp.int32)[None, :]
    row_slot = jnp.sum(jnp.where(id_match, adapter_slot[None, :], 0), axis=1)
    owner_index = tensor_idx * n_pool + pool_idx
    own_slots = owner_index * slots_per_device + jnp.arange(slots_per_device, dtype=jnp.int32)
    own_mask = (row_slot[:, None] == own_slots[None, :]).astype(jnp.float32)
    flat_rows = gathered.reshape(-1, width_of_model)
    down_flattened = adapter_down_weight.reshape(
        slots_per_device * adapter_rank_size, width_of_model
    )
    projected = lax.dot_general(
        flat_rows, down_flattened, (((1,), (1,)), ((), ())), preferred_element_type=jnp.float32
    )
    masked = (
        projected.reshape(-1, step_count, slots_per_device, adapter_rank_size)
        * own_mask[:, None, :, None]
    )
    base_rows = gathered.reshape(tensor_count, n_pool, req_dev * step_count, width_of_model)
    own_group = lax.dynamic_index_in_dim(base_rows, pool_idx, 1, keepdims=False).reshape(
        group_rows, width_of_model
    )
    base_query = jnp.dot(own_group, query_matrix, preferred_element_type=jnp.float32)
    low_rows = masked.astype(jnp.bfloat16).reshape(
        tensor_count, n_pool, req_dev * step_count, slots_per_device * adapter_rank_size
    )
    by_group = jnp.transpose(low_rows, (1, 0, 2, 3)).reshape(
        n_pool, group_rows, slots_per_device * adapter_rank_size
    )
    up_weight_blocks = adapter_up_weight.reshape(
        slots_per_device * adapter_rank_size, tensor_count, head_column_block
    )
    block_count = group_rows * lax.axis_size(("tensor", "pool")) // group_rows
    block_index = jnp.arange(block_count, dtype=jnp.int32)
    head_block = block_index // n_pool
    group_index = block_index % n_pool
    picked_rows = jnp.take(by_group, group_index, axis=0)
    picked_cols = jnp.take(up_weight_blocks, head_block, axis=1)
    partial_sum = jnp.einsum(
        "brk,kbc->brc", picked_rows, picked_cols, preferred_element_type=jnp.float32
    )
    low_delta = lax.psum_scatter(
        partial_sum.reshape(block_count * group_rows, head_column_block),
        ("tensor", "pool"),
        scatter_dimension=0,
        tiled=True,
    )
    queries = (base_query + low_delta).astype(jnp.bfloat16)
    regrouped = lax.all_to_all(
        queries.reshape(tensor_count, req_dev * step_count, head_column_block),
        "tensor",
        split_axis=0,
        concat_axis=2,
        tiled=True,
    )
    return attend(regrouped, cached_key_value, fresh_key_value, cached_length)

def fused(
    dims,
    hidden_ref, matrix_ref, down_ref, up_ref, adapter_ref, table_ref, cache_ref, fresh_ref, length_ref,
    out_ref,
    gath, matrix_v, down_v, up_v, cache_v, hidden_v, fresh_v, adapter_s, table_s, length_s,
    exch_out, exch_in, delta_out, delta_in,
    load_sem, small_sem, z_send, z_recv, f_send, f_recv,
    x_send, x_recv, d_send, d_recv,
):
    T, NC = dims.tensor, dims.chunks
    R = 2 * T
    steps, width = hidden_ref.shape[1], hidden_ref.shape[2]
    rows = R * steps
    part = width // NC
    lanes = part // 4
    half = matrix_v.shape[1]
    span = half * 2
    slot_count, rank = down_ref.shape[0], down_ref.shape[1]
    kvw = cache_ref.shape[3]
    cache_size = cache_ref.shape[2]
    t = lax.axis_index("tensor")
    p = lax.axis_index("pool")
    other = 1 - p
    me = t * 2 + p

    def up_t(j):
        return lax.rem(t + j, T)

    def down_t(j):
        return lax.rem(t + T - j, T)

    def remote(src, dst, ssem, rsem, tt, pp):
        return pltpu.make_async_remote_copy(
            src_ref=src, dst_ref=dst, send_sem=ssem, recv_sem=rsem,
            device_id={"tensor": tt, "pool": pp}, device_id_type=MESH,
        )

    smalls = [
        pltpu.make_async_copy(src, dst, small_sem.at[n])
        for n, (src, dst) in enumerate(
            (
                (hidden_ref.at[0], hidden_v),
                (adapter_ref, adapter_s),
                (table_ref, table_s),
                (fresh_ref.at[0], fresh_v),
                (length_ref, length_s),
            )
        )
    ]
    for load in smalls:
        load.start()
    mat_cols = pl.ds(pl.multiple_of(p * half, half), half)
    mat_loads, down_loads = [], []
    for c in range(NC):
        ks = pl.ds(c * part, part)
        mat_loads.append(pltpu.make_async_copy(matrix_ref.at[ks, mat_cols], matrix_v.at[ks], load_sem.at[2 * c]))
        down_loads.append(pltpu.make_async_copy(down_ref.at[:, :, ks], down_v.at[:, :, ks], load_sem.at[2 * c + 1]))
        mat_loads[c].start()
        down_loads[c].start()
    up_load = pltpu.make_async_copy(up_ref, up_v, load_sem.at[2 * NC])
    cache_load = pltpu.make_async_copy(cache_ref.at[0], cache_v, load_sem.at[2 * NC + 1])
    up_load.start()
    cache_load.start()

    barrier = pltpu.get_barrier_semaphore()
    for j in range(T):
        for q in range(2):
            if j or q:
                pl.semaphore_signal(
                    barrier, inc=1, device_id={"tensor": up_t(j), "pool": other if q else p}, device_id_type=MESH
                )

    smalls[0].wait()
    own = hidden_v[...].astype(jnp.float32)
    for c in range(NC):
        pieces = [own[:, c * part + q * lanes : c * part + (q + 1) * lanes] for q in range(4)]
        gath[c, 0, :, :lanes] = jnp.concatenate(pieces, axis=0).astype(jnp.bfloat16)
    smalls[1].wait()
    smalls[2].wait()
    slot_block = jnp.full((4 * steps, 128), table_s[adapter_s[0]], jnp.int32).astype(jnp.float32).astype(jnp.bfloat16)
    for c in range(NC):
        gath[c, 0, :, lanes:] = slot_block

    pl.semaphore_wait(barrier, R - 1)

    pending = []
    zc, fc = {}, {}
    for c in range(NC):
        for j in range(1, T):
            zc[c, j] = remote(gath.at[c, 0], gath.at[c, 2 * j], z_send.at[c, j], z_recv.at[c, j], up_t(j), p)
            zc[c, j].start()
            pending.append(zc[c, j])
        for j in range(T):
            fc[c, j] = remote(gath.at[c, 2 * j], gath.at[c, 2 * j + 1], f_send.at[c, j], f_recv.at[c, j], t, other)
            pending.append(fc[c, j])
        fc[c, 0].start()
    i0 = lax.broadcasted_iota(jnp.int32, (4 * rows, 4 * rows), 0)
    i1 = lax.broadcasted_iota(jnp.int32, (4 * rows, 4 * rows), 1)
    q0 = lax.div(i0, rows)
    r0 = lax.div(lax.rem(i0, rows), steps)
    s0 = lax.rem(i0, steps)
    order = jnp.where(i1 == r0 * (4 * steps) + q0 * steps + s0, 1.0, 0.0).astype(jnp.bfloat16)

    smalls[3].wait()
    smalls[4].wait()
    fresh = fresh_v[...].astype(jnp.float32)
    pad = jnp.zeros((128 - steps, kvw), jnp.float32)
    fresh_keys = jnp.concatenate([fresh[0], pad], axis=0).astype(jnp.bfloat16)
    fresh_vals = jnp.concatenate([fresh[1], pad], axis=0).astype(jnp.bfloat16)

    base = jnp.zeros((rows, half), jnp.float32)
    low_t = jnp.zeros((slot_count * rank, rows), jnp.float32)
    for c in range(NC):
        for j in range(1, T):
            zc[c, j].wait_recv()
            fc[c, j].start()
        for j in range(T):
            fc[c, j].wait_recv()
        mat_loads[c].wait()
        down_loads[c].wait()
        arrived = gath[c, :, :, :lanes].reshape(R * 4 * steps, lanes)
        ordered = jnp.dot(order, arrived, preferred_element_type=jnp.float32).astype(jnp.bfloat16)
        for q in range(4):
            lhs = ordered[q * rows : (q + 1) * rows]
            k0 = c * part + q * lanes
            dn = down_v[:, :, k0 : k0 + lanes].reshape(slot_count * rank, lanes)
            low_t += lax.dot_general(dn, lhs, (((1,), (1,)), ((), ())), preferred_element_type=jnp.float32)
            base += jnp.dot(lhs, matrix_v[k0 : k0 + lanes, :], preferred_element_type=jnp.float32)

    ri = lax.broadcasted_iota(jnp.int32, (rows, 128), 0)
    row_slot = jnp.zeros((rows, 128), jnp.float32)
    for r in range(R):
        here = (ri >= r * steps) & (ri < (r + 1) * steps)
        row_slot = jnp.where(here, jnp.broadcast_to(gath[0, r, :, lanes:].astype(jnp.float32)[0:1], (rows, 128)), row_slot)
    low = low_t.T
    bits = []
    for n in range(slot_count * rank // 128):
        col_slot = me * slot_count + lax.div(lax.broadcasted_iota(jnp.int32, (rows, 128), 1) + n * 128, rank)
        bits.append(jnp.where(row_slot == col_slot.astype(jnp.float32), low[:, n * 128 : (n + 1) * 128], 0.0))
    low = jnp.concatenate(bits, axis=1).astype(jnp.bfloat16)

    up_load.wait()
    base_wide = jnp.concatenate([jnp.where(p == 0, base, 0.0), jnp.where(p == 1, base, 0.0)], axis=1)
    deltas = []
    for k in range(T):
        upk = up_v[:, :, k * span : (k + 1) * span].reshape(slot_count * rank, span)
        delta = jnp.dot(low, upk, preferred_element_type=jnp.float32)
        deltas.append(delta + jnp.where(t == k, base_wide, 0.0))

    def block_of(r):
        return jnp.concatenate([d[r * steps : (r + 1) * steps] for d in deltas], axis=0)

    order_j = list(range(1, T)) + [0]
    xc, dc = {}, {}
    for j in order_j:
        exch_out[j] = (block_of(2 * j + 1)).astype(LINK)
        xc[j] = remote(exch_out.at[j], exch_in.at[j], x_send.at[j], x_recv.at[j], t, other)
        xc[j].start()
        pending.append(xc[j])
    mine = {j: block_of(2 * j) for j in order_j}
    for j in order_j:
        xc[j].wait_recv()
        both = mine[j] + exch_in[j].astype(jnp.float32)
        if j:
            delta_out[j] = both.astype(LINK)
            dc[j] = remote(delta_out.at[j], delta_in.at[j], d_send.at[j], d_recv.at[j], down_t(j), p)
            dc[j].start()
            pending.append(dc[j])
        else:
            total = both

    cache_load.wait()
    for j in range(1, T):
        dc[j].wait_recv()
        total = total + delta_in[j].astype(jnp.float32)
    queries = total.astype(jnp.bfloat16).astype(jnp.float32)

    groups = span // HEAD_WIDTH
    heads = groups * steps
    scale = 1.0 / math.sqrt(HEAD_WIDTH)
    length = length_s[0]
    old_ok = lax.broadcasted_iota(jnp.int32, (heads, cache_size), 1) < length
    step_of = lax.rem(lax.broadcasted_iota(jnp.int32, (heads, 128), 0), steps)
    new_ok = lax.broadcasted_iota(jnp.int32, (heads, 128), 1) <= step_of
    nt = (((1,), (1,)), ((), ()))
    lanes_of = [slice(k * HEAD_WIDTH, (k + 1) * HEAD_WIDTH) for k in range(T)]
    olds, news = [], []
    for k in range(T):
        rows_k = queries[k * steps : (k + 1) * steps]
        qk = jnp.concatenate(
            [rows_k[:, g * HEAD_WIDTH : (g + 1) * HEAD_WIDTH] for g in range(groups)], axis=0
        ).astype(jnp.bfloat16)
        old = lax.dot_general(qk, cache_v[0, :, lanes_of[k]], nt, preferred_element_type=jnp.float32) * scale
        new = lax.dot_general(qk, fresh_keys[:, lanes_of[k]], nt, preferred_element_type=jnp.float32) * scale
        olds.append(jnp.where(old_ok, old, -1e30))
        news.append(jnp.where(new_ok, new, -1e30))
    old = jnp.concatenate(olds, axis=0)
    new = jnp.concatenate(news, axis=0)
    top = jnp.maximum(jnp.max(old, axis=1, keepdims=True), jnp.max(new, axis=1, keepdims=True))
    old = jnp.exp(old - top)
    new = jnp.exp(new - top)
    inv = 1.0 / (jnp.sum(old, axis=1, keepdims=True) + jnp.sum(new, axis=1, keepdims=True))
    old = (old * inv).astype(jnp.bfloat16)
    new = (new * inv).astype(jnp.bfloat16)
    sums = []
    for k in range(T):
        here = slice(k * heads, (k + 1) * heads)
        res = jnp.dot(old[here], cache_v[1, :, lanes_of[k]], preferred_element_type=jnp.float32)
        res += jnp.dot(new[here], fresh_vals[:, lanes_of[k]], preferred_element_type=jnp.float32)
        sums += [res[g * steps : (g + 1) * steps] for g in range(groups)]
    out_ref[0] = jnp.concatenate(sums, axis=1).astype(jnp.bfloat16)

    for x in pending:
        x.wait_send()


class Dims(NamedTuple):
    tensor: int
    chunks: int


def fused_call(
    hidden_input, query_matrix, adapter_down_weight, adapter_up_weight,
    request_adapter, adapter_slot, cached_key_value, fresh_key_value, cached_length,
):
    T = lax.axis_size("tensor")
    NC = CHUNKS
    R = 2 * T
    steps, width = hidden_input.shape[1], hidden_input.shape[2]
    lanes = width // NC // 4
    half = query_matrix.shape[1] // 2
    span = half * 2
    bf, f32 = jnp.bfloat16, jnp.float32
    V, S = pltpu.VMEM, pltpu.SemaphoreType.DMA
    vm, hb = (pl.BlockSpec(memory_space=m) for m in (pltpu.VMEM, pl.ANY))
    M = pltpu.SMEM
    return pl.pallas_call(
        functools.partial(fused, Dims(T, NC)),
        out_shape=jax.ShapeDtypeStruct((1, steps, span * T), bf),
        in_specs=[hb] * 9,
        out_specs=vm,
        scratch_shapes=[
            V((NC, R, 4 * steps, lanes + 128), bf),
            V((width, half), bf),
            V(adapter_down_weight.shape, bf),
            V(adapter_up_weight.shape, bf),
            V(cached_key_value.shape[1:], bf),
            V(hidden_input.shape[1:], bf),
            V(fresh_key_value.shape[1:], bf),
            M((1,), jnp.int32),
            M(adapter_slot.shape, jnp.int32),
            M((1,), jnp.int32),
            V((T, T * steps, span), LINK),
            V((T, T * steps, span), LINK),
            V((T, T * steps, span), LINK),
            V((T, T * steps, span), LINK),
            S((2 * NC + 2,)),
            S((5,)),
            S((NC, T)), S((NC, T)), S((NC, T)), S((NC, T)),
            S((T,)), S((T,)), S((T,)), S((T,)),
        ],
        compiler_params=pltpu.CompilerParams(
            collective_id=0, has_side_effects=True, vmem_limit_bytes=62 * 1024 * 1024
        ),
        cost_estimate=pl.CostEstimate(flops=10**9, bytes_accessed=16 * 10**6, transcendentals=10**5),
    )(
        hidden_input, query_matrix, adapter_down_weight, adapter_up_weight,
        request_adapter, adapter_slot, cached_key_value, fresh_key_value, cached_length,
    )


def fits_fused(hidden, matrix, down, cache):
    return (
        lax.axis_size("tensor") == KVH
        and lax.axis_size("pool") == 2
        and hidden.shape[0] == 1
        and hidden.shape[1] == 4
        and matrix.shape[1] == QUERY_HEADS // KVH * HEAD_WIDTH
        and (down.shape[0] * down.shape[1]) % 128 == 0
        and down.shape[0] * 2 * KVH <= 256
        and hidden.shape[2] % (CHUNKS * 4 * 128) == 0
        and cache.shape[2] % 128 == 0
    )

def either(*arrays):
    hidden, matrix, down, cache = arrays[0], arrays[1], arrays[2], arrays[6]
    if fits_fused(hidden, matrix, down, cache):
        return fused_call(*arrays)
    return per_device(*arrays)


def solution(mesh):
    placed = (
        P(("groups", "tensor", "batch", "pool"), None, None),
        P(None, "tensor"),
        P(("tensor", "pool"), None, None),
        P(("tensor", "pool"), None, None),
        P(("groups", "tensor", "batch", "pool")),
        P(),
        P(("groups", "tensor", "batch", "pool"), None, None, None),
        P(("groups", "tensor", "batch", "pool"), None, None, None),
        P(("groups", "tensor", "batch", "pool")),
    )
    return jax.shard_map(
        either,
        mesh=mesh,
        in_specs=placed,
        out_specs=P(("groups", "tensor", "batch", "pool"), None, None),
        check_vma=False,
    )
```

```python
import functools
import math
from typing import NamedTuple

import jax
import jax.numpy as jnp
from jax import lax
from jax.experimental import pallas as pl
from jax.experimental.pallas import tpu as pltpu
from jax.sharding import PartitionSpec as P

QUERY_HEADS = 32
KVH = 4
HEAD_WIDTH = 128
CHUNKS = 2
LINK = jnp.float32
MESH = pl.DeviceIdType.MESH


def attend(queries, cached_key_value, fresh_key_value, cached_length):
    req_count = queries.shape[0]
    step_count = queries.shape[1]
    cache_size = cached_key_value.shape[2]
    group_size = QUERY_HEADS // KVH
    head_rows = queries.reshape(req_count, step_count, KVH, group_size, HEAD_WIDTH)
    cache_keys = cached_key_value[:, 0].reshape(req_count, cache_size, KVH, HEAD_WIDTH)
    cache_values = cached_key_value[:, 1].reshape(req_count, cache_size, KVH, HEAD_WIDTH)
    new_keys = fresh_key_value[:, 0].reshape(req_count, step_count, KVH, HEAD_WIDTH)
    new_values = fresh_key_value[:, 1].reshape(req_count, step_count, KVH, HEAD_WIDTH)
    score_scale = 1.0 / math.sqrt(HEAD_WIDTH)
    cached_scores = (
        jnp.einsum("rskgd,rlkd->rkgsl", head_rows, cache_keys, preferred_element_type=jnp.float32)
        * score_scale
    )
    fresh_scores = (
        jnp.einsum("rskgd,rtkd->rkgst", head_rows, new_keys, preferred_element_type=jnp.float32)
        * score_scale
    )
    valid_old = (jnp.arange(cache_size, dtype=jnp.int32)[None, :] < cached_length[:, None])[
        :, None, None, None, :
    ]
    valid_new = (
        jnp.arange(step_count, dtype=jnp.int32)[None, :]
        <= jnp.arange(step_count, dtype=jnp.int32)[:, None]
    )[None, None, None]
    cached_scores = jnp.where(valid_old, cached_scores, -1e30)
    fresh_scores = jnp.where(valid_new, fresh_scores, -1e30)
    row_max = jnp.maximum(jnp.max(cached_scores, axis=-1), jnp.max(fresh_scores, axis=-1))[
        ..., None
    ]
    exp_cached = jnp.exp(cached_scores - row_max)
    exp_fresh = jnp.exp(fresh_scores - row_max)
    denominator = jnp.sum(exp_cached, axis=-1, keepdims=True) + jnp.sum(
        exp_fresh, axis=-1, keepdims=True
    )
    weight_cached = (exp_cached / denominator).astype(jnp.bfloat16)
    weight_fresh = (exp_fresh / denominator).astype(jnp.bfloat16)
    combined = jnp.einsum(
        "rkgsl,rlkd->rskgd", weight_cached, cache_values, preferred_element_type=jnp.float32
    )
    combined = combined + jnp.einsum(
        "rkgst,rtkd->rskgd", weight_fresh, new_values, preferred_element_type=jnp.float32
    )
    return combined.reshape(req_count, step_count, QUERY_HEADS * HEAD_WIDTH).astype(jnp.bfloat16)


def per_device(
    hidden_input,
    query_matrix,
    adapter_down_weight,
    adapter_up_weight,
    request_adapter,
    adapter_slot,
    cached_key_value,
    fresh_key_value,
    cached_length,
):
    req_dev = hidden_input.shape[0]
    step_count = hidden_input.shape[1]
    width_of_model = hidden_input.shape[2]
    tensor_count = lax.axis_size("tensor")
    n_pool = lax.axis_size("pool")
    tensor_idx = lax.axis_index("tensor")
    pool_idx = lax.axis_index("pool")
    slots_per_device = adapter_up_weight.shape[0]
    adapter_rank_size = adapter_up_weight.shape[1]
    head_column_block = query_matrix.shape[1]
    group_rows = tensor_count * req_dev * step_count
    gathered, group_ids = (
        lax.all_gather(hidden_input, ("tensor", "pool"), axis=0, tiled=True),
        lax.all_gather(request_adapter, ("tensor", "pool"), axis=0, tiled=True),
    )
    adapters = adapter_slot.shape[0]
    id_match = group_ids[:, None] == jnp.arange(adapters, dtype=jnp.int32)[None, :]
    row_slot = jnp.sum(jnp.where(id_match, adapter_slot[None, :], 0), axis=1)
    owner_index = tensor_idx * n_pool + pool_idx
    own_slots = owner_index * slots_per_device + jnp.arange(slots_per_device, dtype=jnp.int32)
    own_mask = (row_slot[:, None] == own_slots[None, :]).astype(jnp.float32)
    flat_rows = gathered.reshape(-1, width_of_model)
    down_flattened = adapter_down_weight.reshape(
        slots_per_device * adapter_rank_size, width_of_model
    )
    projected = lax.dot_general(
        flat_rows, down_flattened, (((1,), (1,)), ((), ())), preferred_element_type=jnp.float32
    )
    masked = (
        projected.reshape(-1, step_count, slots_per_device, adapter_rank_size)
        * own_mask[:, None, :, None]
    )
    base_rows = gathered.reshape(tensor_count, n_pool, req_dev * step_count, width_of_model)
    own_group = lax.dynamic_index_in_dim(base_rows, pool_idx, 1, keepdims=False).reshape(
        group_rows, width_of_model
    )
    base_query = jnp.dot(own_group, query_matrix, preferred_element_type=jnp.float32)
    low_rows = masked.astype(jnp.bfloat16).reshape(
        tensor_count, n_pool, req_dev * step_count, slots_per_device * adapter_rank_size
    )
    by_group = jnp.transpose(low_rows, (1, 0, 2, 3)).reshape(
        n_pool, group_rows, slots_per_device * adapter_rank_size
    )
    up_weight_blocks = adapter_up_weight.reshape(
        slots_per_device * adapter_rank_size, tensor_count, head_column_block
    )
    block_count = group_rows * lax.axis_size(("tensor", "pool")) // group_rows
    block_index = jnp.arange(block_count, dtype=jnp.int32)
    head_block = block_index // n_pool
    group_index = block_index % n_pool
    picked_rows = jnp.take(by_group, group_index, axis=0)
    picked_cols = jnp.take(up_weight_blocks, head_block, axis=1)
    partial_sum = jnp.einsum(
        "brk,kbc->brc", picked_rows, picked_cols, preferred_element_type=jnp.float32
    )
    low_delta = lax.psum_scatter(
        partial_sum.reshape(block_count * group_rows, head_column_block),
        ("tensor", "pool"),
        scatter_dimension=0,
        tiled=True,
    )
    queries = (base_query + low_delta).astype(jnp.bfloat16)
    regrouped = lax.all_to_all(
        queries.reshape(tensor_count, req_dev * step_count, head_column_block),
        "tensor",
        split_axis=0,
        concat_axis=2,
        tiled=True,
    )
    return attend(regrouped, cached_key_value, fresh_key_value, cached_length)

def fused(
    dims,
    hidden_ref, matrix_ref, down_ref, up_ref, adapter_ref, table_ref, cache_ref, fresh_ref, length_ref,
    out_ref,
    gath, matrix_v, down_v, up_v, cache_v, hidden_v, fresh_v, adapter_s, table_s, length_s,
    exch_out, exch_in, delta_out, delta_in,
    load_sem, small_sem, z_send, z_recv, f_send, f_recv,
    x_send, x_recv, d_send, d_recv,
):
    T, NC = dims.tensor, dims.chunks
    R = 2 * T
    steps, width = hidden_ref.shape[1], hidden_ref.shape[2]
    rows = R * steps
    part = width // NC
    lanes = part // 4
    half = matrix_v.shape[1]
    span = half * 2
    slot_count, rank = down_ref.shape[0], down_ref.shape[1]
    kvw = cache_ref.shape[3]
    cache_size = cache_ref.shape[2]
    t = lax.axis_index("tensor")
    p = lax.axis_index("pool")
    other = 1 - p
    me = t * 2 + p

    def up_t(j):
        return lax.rem(t + j, T)

    def down_t(j):
        return lax.rem(t + T - j, T)

    def remote(src, dst, ssem, rsem, tt, pp):
        return pltpu.make_async_remote_copy(
            src_ref=src, dst_ref=dst, send_sem=ssem, recv_sem=rsem,
            device_id={"tensor": tt, "pool": pp}, device_id_type=MESH,
        )

    smalls = [
        pltpu.make_async_copy(src, dst, small_sem.at[n])
        for n, (src, dst) in enumerate(
            (
                (hidden_ref.at[0], hidden_v),
                (adapter_ref, adapter_s),
                (table_ref, table_s),
                (fresh_ref.at[0], fresh_v),
                (length_ref, length_s),
            )
        )
    ]
    for load in smalls:
        load.start()
    mat_cols = pl.ds(pl.multiple_of(p * half, half), half)
    mat_loads, down_loads = [], []
    for c in range(NC):
        ks = pl.ds(c * part, part)
        mat_loads.append(pltpu.make_async_copy(matrix_ref.at[ks, mat_cols], matrix_v.at[ks], load_sem.at[2 * c]))
        down_loads.append(pltpu.make_async_copy(down_ref.at[:, :, ks], down_v.at[:, :, ks], load_sem.at[2 * c + 1]))
        mat_loads[c].start()
        down_loads[c].start()
    up_load = pltpu.make_async_copy(up_ref, up_v, load_sem.at[2 * NC])
    cache_load = pltpu.make_async_copy(cache_ref.at[0], cache_v, load_sem.at[2 * NC + 1])
    up_load.start()
    cache_load.start()

    barrier = pltpu.get_barrier_semaphore()
    for j in range(T):
        for q in range(2):
            if j or q:
                pl.semaphore_signal(
                    barrier, inc=1, device_id={"tensor": up_t(j), "pool": other if q else p}, device_id_type=MESH
                )

    smalls[0].wait()
    own = hidden_v[...].astype(jnp.float32)
    for c in range(NC):
        pieces = [own[:, c * part + q * lanes : c * part + (q + 1) * lanes] for q in range(4)]
        gath[c, 0, :, :lanes] = jnp.concatenate(pieces, axis=0).astype(jnp.bfloat16)
    smalls[1].wait()
    smalls[2].wait()
    slot_block = jnp.full((4 * steps, 128), table_s[adapter_s[0]], jnp.int32).astype(jnp.float32).astype(jnp.bfloat16)
    for c in range(NC):
        gath[c, 0, :, lanes:] = slot_block

    pl.semaphore_wait(barrier, R - 1)

    pending = []
    zc, fc = {}, {}
    for c in range(NC):
        for j in range(1, T):
            zc[c, j] = remote(gath.at[c, 0], gath.at[c, 2 * j], z_send.at[c, j], z_recv.at[c, j], up_t(j), p)
            zc[c, j].start()
            pending.append(zc[c, j])
        for j in range(T):
            fc[c, j] = remote(gath.at[c, 2 * j], gath.at[c, 2 * j + 1], f_send.at[c, j], f_recv.at[c, j], t, other)
            pending.append(fc[c, j])
        fc[c, 0].start()
    i0 = lax.broadcasted_iota(jnp.int32, (4 * rows, 4 * rows), 0)
    i1 = lax.broadcasted_iota(jnp.int32, (4 * rows, 4 * rows), 1)
    q0 = lax.div(i0, rows)
    r0 = lax.div(lax.rem(i0, rows), steps)
    s0 = lax.rem(i0, steps)
    order = jnp.where(i1 == r0 * (4 * steps) + q0 * steps + s0, 1.0, 0.0).astype(jnp.bfloat16)

    smalls[3].wait()
    smalls[4].wait()
    fresh = fresh_v[...].astype(jnp.float32)
    pad = jnp.zeros((128 - steps, kvw), jnp.float32)
    fresh_keys = jnp.concatenate([fresh[0], pad], axis=0).astype(jnp.bfloat16)
    fresh_vals = jnp.concatenate([fresh[1], pad], axis=0).astype(jnp.bfloat16)

    base = jnp.zeros((rows, half), jnp.float32)
    low_t = jnp.zeros((slot_count * rank, rows), jnp.float32)
    for c in range(NC):
        for j in range(1, T):
            zc[c, j].wait_recv()
            fc[c, j].start()
        for j in range(T):
            fc[c, j].wait_recv()
        mat_loads[c].wait()
        down_loads[c].wait()
        arrived = gath[c, :, :, :lanes].reshape(R * 4 * steps, lanes)
        ordered = jnp.dot(order, arrived, preferred_element_type=jnp.float32).astype(jnp.bfloat16)
        for q in range(4):
            lhs = ordered[q * rows : (q + 1) * rows]
            k0 = c * part + q * lanes
            dn = down_v[:, :, k0 : k0 + lanes].reshape(slot_count * rank, lanes)
            low_t += lax.dot_general(dn, lhs, (((1,), (1,)), ((), ())), preferred_element_type=jnp.float32)
            base += jnp.dot(lhs, matrix_v[k0 : k0 + lanes, :], preferred_element_type=jnp.float32)

    ri = lax.broadcasted_iota(jnp.int32, (rows, 128), 0)
    row_slot = jnp.zeros((rows, 128), jnp.float32)
    for r in range(R):
        here = (ri >= r * steps) & (ri < (r + 1) * steps)
        row_slot = jnp.where(here, jnp.broadcast_to(gath[0, r, :, lanes:].astype(jnp.float32)[0:1], (rows, 128)), row_slot)
    low = low_t.T
    bits = []
    for n in range(slot_count * rank // 128):
        col_slot = me * slot_count + lax.div(lax.broadcasted_iota(jnp.int32, (rows, 128), 1) + n * 128, rank)
        bits.append(jnp.where(row_slot == col_slot.astype(jnp.float32), low[:, n * 128 : (n + 1) * 128], 0.0))
    low = jnp.concatenate(bits, axis=1).astype(jnp.bfloat16)

    up_load.wait()
    base_wide = jnp.concatenate([jnp.where(p == 0, base, 0.0), jnp.where(p == 1, base, 0.0)], axis=1)
    deltas = []
    for k in range(T):
        upk = up_v[:, :, k * span : (k + 1) * span].reshape(slot_count * rank, span)
        delta = jnp.dot(low, upk, preferred_element_type=jnp.float32)
        deltas.append(delta + jnp.where(t == k, base_wide, 0.0))

    def block_of(r):
        return jnp.concatenate([d[r * steps : (r + 1) * steps] for d in deltas], axis=0)

    order_j = sorted(range(1, T), key=lambda j: abs(2 * j - T)) + [0]
    xc, dc = {}, {}
    for j in order_j:
        exch_out[j] = (block_of(2 * j + 1)).astype(LINK)
        xc[j] = remote(exch_out.at[j], exch_in.at[j], x_send.at[j], x_recv.at[j], t, other)
        xc[j].start()
        pending.append(xc[j])
    mine = {j: block_of(2 * j) for j in order_j}
    for j in order_j:
        xc[j].wait_recv()
        both = mine[j] + exch_in[j].astype(jnp.float32)
        if j:
            delta_out[j] = both.astype(LINK)
            dc[j] = remote(delta_out.at[j], delta_in.at[j], d_send.at[j], d_recv.at[j], down_t(j), p)
            dc[j].start()
            pending.append(dc[j])
        else:
            total = both

    cache_load.wait()
    for j in range(1, T):
        dc[j].wait_recv()
        total = total + delta_in[j].astype(jnp.float32)
    queries = total.astype(jnp.bfloat16).astype(jnp.float32)

    groups = span // HEAD_WIDTH
    heads = groups * steps
    scale = 1.0 / math.sqrt(HEAD_WIDTH)
    length = length_s[0]
    old_ok = lax.broadcasted_iota(jnp.int32, (heads, cache_size), 1) < length
    step_of = lax.rem(lax.broadcasted_iota(jnp.int32, (heads, 128), 0), steps)
    new_ok = lax.broadcasted_iota(jnp.int32, (heads, 128), 1) <= step_of
    nt = (((1,), (1,)), ((), ()))
    lanes_of = [slice(k * HEAD_WIDTH, (k + 1) * HEAD_WIDTH) for k in range(T)]
    olds, news = [], []
    for k in range(T):
        rows_k = queries[k * steps : (k + 1) * steps]
        qk = jnp.concatenate(
            [rows_k[:, g * HEAD_WIDTH : (g + 1) * HEAD_WIDTH] for g in range(groups)], axis=0
        ).astype(jnp.bfloat16)
        old = lax.dot_general(qk, cache_v[0, :, lanes_of[k]], nt, preferred_element_type=jnp.float32) * scale
        new = lax.dot_general(qk, fresh_keys[:, lanes_of[k]], nt, preferred_element_type=jnp.float32) * scale
        olds.append(jnp.where(old_ok, old, -1e30))
        news.append(jnp.where(new_ok, new, -1e30))
    old = jnp.concatenate(olds, axis=0)
    new = jnp.concatenate(news, axis=0)
    top = jnp.maximum(jnp.max(old, axis=1, keepdims=True), jnp.max(new, axis=1, keepdims=True))
    old = jnp.exp(old - top)
    new = jnp.exp(new - top)
    inv = 1.0 / (jnp.sum(old, axis=1, keepdims=True) + jnp.sum(new, axis=1, keepdims=True))
    old = (old * inv).astype(jnp.bfloat16)
    new = (new * inv).astype(jnp.bfloat16)
    sums = []
    for k in range(T):
        here = slice(k * heads, (k + 1) * heads)
        res = jnp.dot(old[here], cache_v[1, :, lanes_of[k]], preferred_element_type=jnp.float32)
        res += jnp.dot(new[here], fresh_vals[:, lanes_of[k]], preferred_element_type=jnp.float32)
        sums += [res[g * steps : (g + 1) * steps] for g in range(groups)]
    out_ref[0] = jnp.concatenate(sums, axis=1).astype(jnp.bfloat16)

    for x in pending:
        x.wait_send()


class Dims(NamedTuple):
    tensor: int
    chunks: int


def fused_call(
    hidden_input, query_matrix, adapter_down_weight, adapter_up_weight,
    request_adapter, adapter_slot, cached_key_value, fresh_key_value, cached_length,
):
    T = lax.axis_size("tensor")
    NC = CHUNKS
    R = 2 * T
    steps, width = hidden_input.shape[1], hidden_input.shape[2]
    lanes = width // NC // 4
    half = query_matrix.shape[1] // 2
    span = half * 2
    bf, f32 = jnp.bfloat16, jnp.float32
    V, S = pltpu.VMEM, pltpu.SemaphoreType.DMA
    vm, hb = (pl.BlockSpec(memory_space=m) for m in (pltpu.VMEM, pl.ANY))
    M = pltpu.SMEM
    return pl.pallas_call(
        functools.partial(fused, Dims(T, NC)),
        out_shape=jax.ShapeDtypeStruct((1, steps, span * T), bf),
        in_specs=[hb] * 9,
        out_specs=vm,
        scratch_shapes=[
            V((NC, R, 4 * steps, lanes + 128), bf),
            V((width, half), bf),
            V(adapter_down_weight.shape, bf),
            V(adapter_up_weight.shape, bf),
            V(cached_key_value.shape[1:], bf),
            V(hidden_input.shape[1:], bf),
            V(fresh_key_value.shape[1:], bf),
            M((1,), jnp.int32),
            M(adapter_slot.shape, jnp.int32),
            M((1,), jnp.int32),
            V((T, T * steps, span), LINK),
            V((T, T * steps, span), LINK),
            V((T, T * steps, span), LINK),
            V((T, T * steps, span), LINK),
            S((2 * NC + 2,)),
            S((5,)),
            S((NC, T)), S((NC, T)), S((NC, T)), S((NC, T)),
            S((T,)), S((T,)), S((T,)), S((T,)),
        ],
        compiler_params=pltpu.CompilerParams(
            collective_id=0, has_side_effects=True, vmem_limit_bytes=62 * 1024 * 1024
        ),
        cost_estimate=pl.CostEstimate(flops=10**9, bytes_accessed=16 * 10**6, transcendentals=10**5),
    )(
        hidden_input, query_matrix, adapter_down_weight, adapter_up_weight,
        request_adapter, adapter_slot, cached_key_value, fresh_key_value, cached_length,
    )


def fits_fused(hidden, matrix, down, cache):
    return (
        lax.axis_size("tensor") == KVH
        and lax.axis_size("pool") == 2
        and hidden.shape[0] == 1
        and hidden.shape[1] == 4
        and matrix.shape[1] == QUERY_HEADS // KVH * HEAD_WIDTH
        and (down.shape[0] * down.shape[1]) % 128 == 0
        and down.shape[0] * 2 * KVH <= 256
        and hidden.shape[2] % (CHUNKS * 4 * 128) == 0
        and cache.shape[2] % 128 == 0
    )

def either(*arrays):
    hidden, matrix, down, cache = arrays[0], arrays[1], arrays[2], arrays[6]
    if fits_fused(hidden, matrix, down, cache):
        return fused_call(*arrays)
    return per_device(*arrays)


def solution(mesh):
    placed = (
        P(("groups", "tensor", "batch", "pool"), None, None),
        P(None, "tensor"),
        P(("tensor", "pool"), None, None),
        P(("tensor", "pool"), None, None),
        P(("groups", "tensor", "batch", "pool")),
        P(),
        P(("groups", "tensor", "batch", "pool"), None, None, None),
        P(("groups", "tensor", "batch", "pool"), None, None, None),
        P(("groups", "tensor", "batch", "pool")),
    )
    return jax.shard_map(
        either,
        mesh=mesh,
        in_specs=placed,
        out_specs=P(("groups", "tensor", "batch", "pool"), None, None),
        check_vma=False,
    )
```
